128 devices in a mesh: ctx: 16 (over x_lo, z, core), head: 8 (over y, x_hi).
Axes of the slice: x: 4 (x_hi: 2, x_lo: 2; x = x_hi * 2 + x_lo), y: 4, z: 4, core: 2. Of those that a mesh axis runs over, the one named last changes fastest.
Arguments:
- states: bfloat16 [16384, 4096], P('ctx'), may hold values from -64 to 64
- seg_ids: int32 [16384], replicated, may hold values from 0 to 3, never falling along the last dimension, each value on 1 to 8192 neighbouring positions
- span_order: int32 [32], replicated, may hold values from 0 to 31, as said below
- w_query: bfloat16 [4096, 2048], P(None, 'head'), may hold values from -0.09375 to 0.09375
- w_key: bfloat16 [4096, 1024], P(None, 'head'), may hold values from -0.09375 to 0.09375
- w_value: bfloat16 [4096, 1024], P(None, 'head'), may hold values from -1.5 to 1.5
- w_out: bfloat16 [2048, 4096], P('head'), may hold values from -0.1875 to 0.1875
Outputs:
- block_out: bfloat16 [16384, 4096], P('ctx', 'head')
The draws below stay inside these ranges and needn't reach their ends.
Inputs may be any that keep to these rules, and one draw needn't show every extreme that they name: `span_order`: each span of 512 positions stands in exactly one slot; the slots 2 d and 2 d + 1 of device d of ctx hold spans i and 31 - i for some i, in either order.
All inputs are finite; a program needn't handle non-finite values.
Results may differ from the reference program's by a relative error of at most 0.019.
Values may be sent and summed in bfloat16 or wider, within the bound.
No kernel may reach another device: no remote copies, remote signals or barrier semaphores. Data moves between devices by JAX's collectives and lax.ppermute only.
A program may use at most 128 MiB of HBM per device.

```python
import math
import jax
import jax.numpy as jnp
import numpy as np
from jax import lax

D = 4096
QH = 16
KVH = 8
HD = 128
SPAN = 512
DOCS = 4
TOKENS = 16384
N_HEAD = 8


def draw_states(key, part):
    key = jax.random.fold_in(key, 11)
    bulk_key = jax.random.fold_in(key, 0)
    bulk = jax.random.normal(bulk_key, (TOKENS, D), jnp.float32)
    return jnp.clip(bulk, -64.0, 64.0).astype(jnp.bfloat16)


def draw_span_order(key, part):
    key = jax.random.fold_in(key, 23)
    pair_count = TOKENS // (2 * SPAN)
    order_key, flip_key = jax.random.split(key)
    holder = jax.random.permutation(order_key, pair_count).astype(jnp.int32)
    flipped = jax.random.randint(flip_key, (pair_count,), 0, 2).astype(jnp.int32)
    early = jnp.arange(pair_count, dtype=jnp.int32)
    late = 2 * pair_count - 1 - early
    result = jnp.zeros((2 * pair_count,), jnp.int32)
    result = result.at[2 * holder + flipped].set(early)
    result = result.at[2 * holder + 1 - flipped].set(late)
    return result


def raised(drawn, own_key, source, target, blocks, factor):
    def block_of(axis_at):
        return (jnp.arange(drawn.shape[axis_at]) // (drawn.shape[axis_at] // blocks)).reshape((-1,) + (1,) * (drawn.ndim - 1 - axis_at))

    first = jax.random.permutation(own_key, blocks)[block_of(target)]
    other_side = (block_of(target) + blocks // 2) % blocks
    return jnp.where((block_of(source) == first) | (block_of(source) == other_side), factor * drawn, drawn)


def levels(key, shape, pieces, smallest, top_value):
    level, own = 1.0, jax.random.fold_in(key, 6)
    for dim, shards_of in pieces:
        steps = jnp.exp(jax.random.uniform(jax.random.fold_in(own, dim), (shards_of,), jnp.float32, smallest / len(pieces), top_value / len(pieces)))
        level = level * jnp.repeat(steps, shape[dim] // shards_of).reshape([-1 if axis == dim else 1 for axis in range(len(shape))])
    return level


def split_up(amount, total, reach, lean):
    weights = [(1 << 20) // math.isqrt(grade ** lean) + 1 for grade in range(2, amount + 1)]
    rest, holding = total - reach - (amount - 1), [1] * (amount - 1)
    while rest > 0:
        movable = [i for i in range(amount - 1) if holding[i] < reach]
        pool, remaining = sum([weights[i] for i in movable]), rest
        for i in movable:
            extra = min(reach - holding[i], max(1, remaining * weights[i] // pool), rest)
            holding[i] = holding[i] + extra
            rest = rest - extra
    return np.array([reach] + holding)


def ragged_sizes(stream_key, count, total, limit, slope):
    if count == 2:
        one = jax.random.randint(stream_key, (), max(1, total - limit), min(limit, total - 1) + 1)
        return jnp.stack([one, total - one])
    tallies = jnp.asarray(split_up(count, total, limit, slope), jnp.int32)
    couples = (count - 1) // 2
    source_of, taker = tallies[1:1 + 2 * couples:2], tallies[2:2 + 2 * couples:2]
    slack = jnp.minimum(source_of - 1, limit - taker)
    passed = jax.random.randint(jax.random.fold_in(stream_key, 1), (couples,), 0, 1 << 20) % (slack + 1)
    tallies = tallies.at[1:1 + 2 * couples:2].set(source_of - passed).at[2:2 + 2 * couples:2].set(taker + passed)
    return tallies[jax.random.permutation(jax.random.fold_in(stream_key, 2), count)]


def scatter_about(key, shape, width, most, shards=(), held_as=jnp.bfloat16):
    entries = jax.random.normal(key, shape, jnp.float32) * width
    if len(shards) > 0:
        entries = levels(key, shape, shards, -0.22, 0.18) * entries
    return jnp.clip(entries, min=-most, max=most).astype(held_as)


def noise_with(key, extent, deviation, reach, shards, heavy, kind=jnp.bfloat16):
    entries = deviation * jax.random.normal(key, extent, jnp.float32)
    if shards:
        entries = entries * levels(key, extent, shards, -0.22, 0.18)
    return jnp.clip(raised(entries, jax.random.fold_in(key, 3), *heavy), -reach, reach).astype(kind)


def setup_inputs(seed: int = 0) -> dict:
    key_list = jax.random.split(jax.random.key(seed), 8)
    return {
        "states": draw_states(jax.random.fold_in(key_list[7], 71), 0),
        "seg_ids": jnp.searchsorted(jnp.cumsum(ragged_sizes(key_list[1], DOCS, TOKENS, TOKENS // 2, 0)), jnp.arange(TOKENS), side="right").astype(jnp.int32),
        "span_order": draw_span_order(jax.random.fold_in(key_list[7], 71), 0),
        "w_query": scatter_about(key_list[3], (D, QH * HD), D ** -0.5, 0.09375, ((1, 8),)),
        "w_key": scatter_about(key_list[4], (D, KVH * HD), D ** -0.5, 0.09375, ((1, 8),)),
        "w_value": scatter_about(key_list[5], (D, KVH * HD), (max(D // 256, 1)) ** -0.5, 1.5, ((1, 8),)),
        "w_out": noise_with(key_list[6], (QH * HD, D), (QH * HD) ** -0.5, 0.1875, ((0, 8),), (0, 1, 8, 2.0)),
    }


rope_base = 500000.0
neg_large = -1e30


def rotate(values, positions):
    middle = values.shape[-1] // 2
    frequency = rope_base ** (-jnp.arange(middle, dtype=jnp.float32) * 2.0 / values.shape[-1])
    angles = positions.astype(jnp.float32)[:, None] * frequency[None, :]
    cos_part = jnp.cos(angles)[:, None, :]
    sin_part = jnp.sin(angles)[:, None, :]
    first_half = values[..., :middle]
    second_half = values[..., middle:]
    return jnp.concatenate([first_half * cos_part - second_half * sin_part, second_half * cos_part + first_half * sin_part], -1)


def reference(states, seg_ids, span_order, w_query, w_key, w_value, w_out):
    total_rows = states.shape[0]
    row_index = jnp.arange(total_rows, dtype=jnp.int32)
    positions = (span_order[row_index // SPAN] * SPAN + row_index % SPAN).astype(jnp.int32)
    segments = seg_ids[positions]
    group_size = QH // KVH
    queries = jnp.dot(states, w_query, preferred_element_type=jnp.float32).reshape(total_rows, QH, HD)
    queries = (rotate(queries, positions) * (HD ** -0.5)).astype(jnp.bfloat16)
    key_rows = jnp.dot(states, w_key, preferred_element_type=jnp.float32).reshape(total_rows, KVH, HD)
    key_rows = rotate(key_rows, positions).astype(jnp.bfloat16)
    value_rows = jnp.dot(states, w_value, preferred_element_type=jnp.float32).astype(jnp.bfloat16).reshape(total_rows, KVH, HD)
    keys_wide = key_rows.astype(jnp.float32)
    values_wide = value_rows.astype(jnp.float32)

    def attend(block_id):
        first_row = (block_id * SPAN).astype(jnp.int32)
        query_block = lax.dynamic_slice_in_dim(queries, first_row, SPAN, 0).astype(jnp.float32).reshape(SPAN, KVH, group_size, HD)
        query_pos = lax.dynamic_slice_in_dim(positions, first_row, SPAN, 0)
        query_seg = lax.dynamic_slice_in_dim(segments, first_row, SPAN, 0)
        scores = jnp.einsum("qkgd,tkd->kgqt", query_block, keys_wide)
        allowed = (positions[None, :] <= query_pos[:, None]) & (segments[None, :] == query_seg[:, None])
        scores = jnp.where(allowed, scores, neg_large)
        row_max = jnp.max(scores, -1, keepdims=True)
        weights = jnp.where(allowed, jnp.exp(scores - row_max), 0.0)
        totals = jnp.sum(weights, -1)
        rounded = lax.optimization_barrier(weights.astype(jnp.bfloat16)).astype(jnp.float32)
        mixture = jnp.einsum("kgqt,tkd->qkgd", rounded, values_wide) / jnp.transpose(totals, (2, 0, 1))[..., None]
        return mixture.reshape(SPAN, QH * HD).astype(jnp.bfloat16)

    attended = lax.map(attend, jnp.arange(total_rows // SPAN, dtype=jnp.int32)).reshape(total_rows, QH * HD)
    per_group = QH * HD // N_HEAD
    summed = jnp.zeros((total_rows, D), jnp.float32)
    for member in range(N_HEAD):
        partial_value = jnp.dot(attended[:, member * per_group:(member + 1) * per_group], w_out[member * per_group:(member + 1) * per_group], preferred_element_type=jnp.float32)
        summed = summed + lax.optimization_barrier(partial_value.astype(jnp.bfloat16)).astype(jnp.float32)
    return summed.astype(jnp.bfloat16)
```

```python
import functools
import math

import jax
import jax.numpy as jnp
import numpy as np
from jax import lax
from jax.experimental import pallas as pl
from jax.experimental.pallas import tpu as pltpu
from jax.sharding import PartitionSpec as P

HD = 128
SPAN = 512
SPANS = 32
rope_base = 500000.0
neg_large = -1e30
F32 = jnp.float32
BF16 = jnp.bfloat16


def rope_tables():
    freq = rope_base ** (-np.arange(64, dtype=np.float64) * 2.0 / HD)
    sign = np.concatenate([-np.ones(64), np.ones(64)])

    def pair(pos):
        ang = np.concatenate([pos[:, None] * freq, pos[:, None] * freq], 1)
        return np.stack([np.cos(ang), np.sin(ang) * sign]).astype(np.float32)

    return pair(np.arange(SPANS) * float(SPAN)), pair(np.arange(SPAN) * 1.0)


def rotated(x, span, big_ref, small_ref):
    cb = big_ref[0, pl.ds(span, 1), :]
    sb = big_ref[1, pl.ds(span, 1), :]
    cs = small_ref[0]
    ss = small_ref[1]
    cos = cb * cs - sb * ss
    sin = (sb * cs + cb * ss)
    return x * cos + pltpu.roll(x, 64, 1) * sin


def kv_kernel(info_ref, x_ref, wk_ref, wv_ref, big_ref, small_ref, out_ref, w_ref):
    g = pl.program_id(0)

    @pl.when(g == 0)
    def _():
        w_ref[:, :HD] = wk_ref[...]
        w_ref[:, HD:] = wv_ref[...]

    y = jnp.dot(x_ref[...], w_ref[...], preferred_element_type=F32)
    out_ref[0:SPAN, :] = rotated(y[:, :HD], info_ref[2 + g], big_ref, small_ref).astype(BF16)
    for c in range(SPAN // HD):
        tile = y[c * HD:(c + 1) * HD, HD:]
        out_ref[SPAN + c * HD:SPAN + (c + 1) * HD, :] = tile.T.astype(BF16)


def q_kernel(info_ref, x_ref, wq_ref, big_ref, small_ref, out_ref):
    g = pl.program_id(0)
    y = jnp.dot(x_ref[...], wq_ref[...], preferred_element_type=F32)
    scale = HD ** (-0.5) * math.log2(math.e)
    for h in range(2):
        r = rotated(y[:, h * HD:(h + 1) * HD], info_ref[2 + g], big_ref, small_ref) * scale
        out_ref[0, :, h * SPAN:(h + 1) * SPAN] = r.T.astype(BF16)


def project(info, states, weights, tables, kernel, out_shape, out_block, out_map, scratch):
    width = states.shape[1]
    whole = lambda a: pl.BlockSpec(a.shape, lambda g, i: (0,) * a.ndim)
    flops = 2 * states.shape[0] * width * sum(w.shape[1] for w in weights)
    return pl.pallas_call(
        kernel,
        grid_spec=pltpu.PrefetchScalarGridSpec(
            num_scalar_prefetch=1,
            grid=(2,),
            in_specs=[pl.BlockSpec((SPAN, width), lambda g, i: (i[g], 0))]
            + [whole(a) for a in (*weights, *tables)],
            out_specs=pl.BlockSpec(out_block, out_map),
            scratch_shapes=scratch,
        ),
        out_shape=jax.ShapeDtypeStruct(out_shape, BF16),
        compiler_params=pltpu.CompilerParams(vmem_limit_bytes=40 * 2**20),
        cost_estimate=pl.CostEstimate(flops=flops, bytes_accessed=12 * 2**20, transcendentals=0),
    )(info, states, *weights, *tables)


def attn_kernel(rels, info_ref, order_ref, *refs):
    n = len(rels)
    kv = refs[:n]
    q_ref, out_ref, kb, vb, m_ref, acc_ref, span_ref, sems = refs[n:]
    me = info_ref[4]
    x0, z0, c0 = me // 8, (me // 2) % 4, me % 2

    copies = []
    for t, (dx, dz, dc) in enumerate(rels):
        for half in range(2):
            u = 2 * t + half
            base = half * 2 * SPAN
            row = [pltpu.make_async_copy(kv[t].at[pl.ds(base, SPAN), :], kb.at[u], sems.at[u, 0])]
            for c in range(4):
                row.append(
                    pltpu.make_async_copy(
                        kv[t].at[pl.ds(base + SPAN + c * HD, HD), :],
                        vb.at[u, pl.ds(0, HD), pl.ds(c * HD, HD)],
                        sems.at[u, 1 + c],
                    )
                )
            for copy in row:
                copy.start()
            copies.append(row)
        who = ((x0 ^ dx) * 4 + ((z0 + dz + 4) % 4)) * 2 + (c0 ^ dc)
        early = jnp.minimum(order_ref[2 * who], order_ref[2 * who + 1])
        span_ref[2 * t] = early
        span_ref[2 * t + 1] = SPANS - 1 - early
    vb[:, HD:, :] = jnp.ones((2 * n, 16, SPAN), BF16)
    m_ref[...] = jnp.full(m_ref.shape, neg_large, F32)
    acc_ref[...] = jnp.zeros(acc_ref.shape, F32)

    def first_of(p):
        low = jnp.int32(0)
        for d in range(3):
            s = info_ref[8 + d]
            low = jnp.where(s <= p, s, low)
        return low

    def block(u, qs, masked):
        k = kb[u]
        v = vb[u]
        qspan = info_ref[2 + qs]
        for qc in range(4):
            sl = slice(qc * 256, (qc + 1) * 256)
            s = jnp.dot(k, q_ref[qs, :, sl], preferred_element_type=F32)
            if masked:
                qpos = lax.broadcasted_iota(jnp.int32, (1, 256), 1) + ((qc % 2) * 256 + qspan * SPAN)
                low = first_of(qpos)
                kpos = lax.broadcasted_iota(jnp.int32, (SPAN, 1), 0) + span_ref[u] * SPAN
                s = jnp.where((kpos <= qpos) & (kpos >= low), s, neg_large)
            old = m_ref[qs, :, sl]
            new = jnp.maximum(old, jnp.max(s, 0, keepdims=True))
            p = jnp.exp2(s - new).astype(BF16)
            m_ref[qs, :, sl] = new
            acc_ref[qs, :, sl] = acc_ref[qs, :, sl] * jnp.exp2(old - new) + jnp.dot(
                v, p, preferred_element_type=F32
            )

    def arrived(u):
        pltpu.make_async_copy(kb.at[u], kb.at[u], sems.at[u, 0]).wait()
        for c in range(4):
            spot = vb.at[u, pl.ds(0, HD), pl.ds(c * HD, HD)]
            pltpu.make_async_copy(spot, spot, sems.at[u, 1 + c]).wait()

    def visit(u, qs):
        qspan = info_ref[2 + qs]
        kspan = span_ref[u]
        low_first = first_of(qspan * SPAN)
        low_last = first_of(qspan * SPAN + SPAN - 1)
        seen = (kspan <= qspan) & (kspan * SPAN + SPAN - 1 >= low_first)
        cut = (kspan == qspan) | (kspan * SPAN < low_last)

        @pl.when(seen & cut)
        def _():
            block(u, qs, True)

        @pl.when(seen & jnp.logical_not(cut))
        def _():
            block(u, qs, False)

    def step(u, carry):
        arrived(u)
        for qs in range(2):
            visit(u, qs)
        return carry

    lax.fori_loop(0, 2 * n, step, 0)

    for qs in range(2):
        for h in range(2):
            sl = slice(h * SPAN, (h + 1) * SPAN)
            value = acc_ref[qs, 0:HD, sl] / acc_ref[qs, HD:HD + 1, sl]
            out_ref[qs, :, h * HD:(h + 1) * HD] = value.T.astype(BF16)


def attend(info, order, units, rels, q):
    n = len(units)
    anywhere = pl.BlockSpec(memory_space=pl.ANY)
    scalar = pl.BlockSpec(memory_space=pltpu.SMEM)
    local = pl.BlockSpec(memory_space=pltpu.VMEM)
    return pl.pallas_call(
        functools.partial(attn_kernel, rels),
        in_specs=[scalar, scalar] + [anywhere] * n + [local],
        out_specs=local,
        out_shape=jax.ShapeDtypeStruct((2, SPAN, 2 * HD), BF16),
        scratch_shapes=[
            pltpu.VMEM((2 * n, SPAN, HD), BF16),
            pltpu.VMEM((2 * n, HD + 16, SPAN), BF16),
            pltpu.VMEM((2, 1, 2 * SPAN), F32),
            pltpu.VMEM((2, HD + 16, 2 * SPAN), F32),
            pltpu.SMEM((2 * n,), jnp.int32),
            pltpu.SemaphoreType.DMA((2 * n, 5)),
        ],
        compiler_params=pltpu.CompilerParams(vmem_limit_bytes=40 * 2**20),
        cost_estimate=pl.CostEstimate(flops=9 * 10**9, bytes_accessed=9 * 2**20, transcendentals=2**24),
    )(info, order, *units, q)


def out_kernel(info_ref, *refs):
    a, w, out_ref = refs[0:4], refs[4:8], refs[8]
    total = None
    for t in range(4):
        part = jnp.dot(a[t][0], w[t][...], preferred_element_type=F32)
        total = part if total is None else total + part
    out_ref[0] = total.astype(out_ref.dtype)


def output(info, parts, weights, dtype):
    cols = weights[0].shape[1]
    return pl.pallas_call(
        out_kernel,
        grid_spec=pltpu.PrefetchScalarGridSpec(
            num_scalar_prefetch=1,
            grid=(2,),
            in_specs=[pl.BlockSpec((1, SPAN, 2 * HD), lambda g, i: (g, 0, 0))] * 4
            + [pl.BlockSpec((2 * HD, cols), lambda g, i: (0, 0))] * 4,
            out_specs=pl.BlockSpec((1, SPAN, cols), lambda g, i: (i[g], 0, 0)),
        ),
        out_shape=jax.ShapeDtypeStruct((2, SPAN, cols), dtype),
        compiler_params=pltpu.CompilerParams(vmem_limit_bytes=40 * 2**20),
        cost_estimate=pl.CostEstimate(flops=1024 * 1024 * cols * 2, bytes_accessed=5 * 2**20, transcendentals=0),
    )(info, *parts, *weights)


def pairs(move):
    out = []
    for x in range(4):
        for y in range(4):
            for z in range(4):
                for c in range(2):
                    def flat(x, y, z, c):
                        x, y, z, c = x % 4, y % 4, z % 4, c % 2
                        return ((x % 2 * 4 + z) * 2 + c) * 8 + y * 2 + x // 2
                    out.append((flat(x, y, z, c), flat(*move(x, y, z, c))))
    return out


to_pair = pairs(lambda x, y, z, c: (x ^ 1, y, z, c))
to_far = pairs(lambda x, y, z, c: (x + 2, y, z, c))
to_core = pairs(lambda x, y, z, c: (x, y, z, c + 1))
z_up = pairs(lambda x, y, z, c: (x, y, z + 1, c))
z_down = pairs(lambda x, y, z, c: (x, y, z - 1, c))
y_up = pairs(lambda x, y, z, c: (x, y + 1, z, c))
y_down = pairs(lambda x, y, z, c: (x, y - 1, z, c))
y_two = pairs(lambda x, y, z, c: (x, y + 2, z, c))


def send(value, to):
    return lax.ppermute(value, ("ctx", "head"), to)


def per_device(states, seg_ids, span_order, w_query, w_key, w_value, w_out):
    me = lax.axis_index("ctx")
    head = lax.axis_index("head")
    y, far = head // 2, head % 2
    mine = lax.dynamic_slice_in_dim(span_order, 2 * me, 2, 0)
    first_early = mine[0] < mine[1]
    early_slot = jnp.where(first_early, 0, 1).astype(jnp.int32)
    early = jnp.minimum(mine[0], mine[1])
    starts = jnp.sum(seg_ids[None, :] < jnp.arange(1, 4, dtype=jnp.int32)[:, None], 1, dtype=jnp.int32)
    head_part = jnp.stack([early_slot, 1 - early_slot, early, SPANS - 1 - early, me.astype(jnp.int32)])
    info = jnp.concatenate([head_part, jnp.zeros((3,), jnp.int32), starts])

    tables = tuple(jnp.asarray(t) for t in rope_tables())
    kv = project(
        head_part, states, (w_key, w_value), tables, kv_kernel, (4 * SPAN, HD), (2 * SPAN, HD),
        lambda g, i: (g, 0), [pltpu.VMEM((states.shape[1], 2 * HD), BF16)],
    )
    q = project(
        head_part, states, (w_query,), tables, q_kernel, (2, HD, 2 * SPAN), (1, HD, 2 * SPAN),
        lambda g, i: (g, 0, 0), [],
    )

    half = 2 * SPAN
    pair = send(kv, to_pair)
    below = send(kv, z_up)
    above = send(kv, z_down)
    pair_below = send(below, to_pair)
    pair_above = send(pair, z_down)
    two = send(below, z_up)
    pair_two = jnp.concatenate([send(pair_below[:half], z_up), send(pair_above[half:], z_down)], 0)
    units = [kv, pair, below, above, pair_below, pair_above, two, pair_two]
    rels = [(0, 0), (1, 0), (0, -1), (0, 1), (1, -1), (1, 1), (0, 2), (1, 2)]
    units = units + [send(u, to_core) for u in units]
    rels = tuple((a, b, 0) for a, b in rels) + tuple((a, b, 1) for a, b in rels)

    wide = w_out.shape[1] // 4
    def columns(step):
        return lax.dynamic_slice_in_dim(w_out, ((y + step) % 4) * wide, wide, 1)
    weights = [columns(0), send(columns(1), y_up), send(columns(3), y_down), send(columns(2), y_two)]

    attended = attend(info, span_order, units, rels, q)

    up = send(attended, y_up)
    down = send(attended, y_down)
    across = jnp.concatenate([send(up[:1], y_up), send(down[1:], y_down)], 0)
    parts = [attended, up, down, across]
    narrow = wide // 2
    theirs = [lax.dynamic_slice_in_dim(w, (1 - far) * narrow, narrow, 1) for w in weights]
    ours = [lax.dynamic_slice_in_dim(w, far * narrow, narrow, 1) for w in weights]
    partial = send(output(head_part, parts, theirs, BF16), to_far)
    own = output(head_part, parts, ours, F32)
    result = (own + partial.astype(F32)).astype(BF16)
    return result.reshape(2 * SPAN, narrow)


def solution(mesh):
    in_specs = (
        P("ctx", None),
        P(),
        P(),
        P(None, "head"),
        P(None, "head"),
        P(None, "head"),
        P("head", None),
    )
    out_specs = P("ctx", "head")
    return jax.shard_map(
        per_device, mesh=mesh, in_specs=in_specs, out_specs=out_specs, check_vma=False
    )
```

```python
import functools
import math

import jax
import jax.numpy as jnp
import numpy as np
from jax import lax
from jax.experimental import pallas as pl
from jax.experimental.pallas import tpu as pltpu
from jax.sharding import PartitionSpec as P

HD = 128
SPAN = 512
SPANS = 32
CHUNKS = 4
rope_base = 500000.0
neg_large = -1e30
F32 = jnp.float32
BF16 = jnp.bfloat16
HBM = pl.BlockSpec(memory_space=pltpu.HBM)
ANYWHERE = pl.BlockSpec(memory_space=pl.ANY)
SCALAR = pl.BlockSpec(memory_space=pltpu.SMEM)
LOCAL = pl.BlockSpec(memory_space=pltpu.VMEM)
LIMIT = pltpu.CompilerParams(vmem_limit_bytes=20 * 2**20)
WIDE = pltpu.CompilerParams(vmem_limit_bytes=57 * 2**20)


def rope_tables():
    freq = rope_base ** (-np.arange(64, dtype=np.float64) * 2.0 / HD)
    sign = np.concatenate([-np.ones(64), np.ones(64)])

    def pair(pos):
        ang = np.concatenate([pos[:, None] * freq, pos[:, None] * freq], 1)
        return np.stack([np.cos(ang), np.sin(ang) * sign]).astype(np.float32)

    return pair(np.arange(SPANS) * float(SPAN)), pair(np.arange(SPAN) * 1.0)


def rotated(x, span, big_ref, small_ref):
    cb = big_ref[0, pl.ds(span, 1), :]
    sb = big_ref[1, pl.ds(span, 1), :]
    cs = small_ref[0]
    ss = small_ref[1]
    cos = cb * cs - sb * ss
    sin = sb * cs + cb * ss
    return x * cos + pltpu.roll(x, 64, 1) * sin


def own_spans(order_ref):
    me = lax.axis_index("ctx")
    a, b = order_ref[2 * me], order_ref[2 * me + 1]
    return jnp.where(a < b, 0, 1).astype(jnp.int32), jnp.minimum(a, b)


def bring(pairs_of_refs, sems, base):
    copies = [pltpu.make_async_copy(a, b, sems.at[base + t]) for t, (a, b) in enumerate(pairs_of_refs)]
    for copy in copies:
        copy.start()
    return copies


def project_kernel(
    order_ref, x_ref, wk_ref, wv_ref, wq_ref, big_ref, small_ref,
    kv_ref, q_ref, x_s, w_s, big_s, small_s, sems,
):
    slot, span = own_spans(order_ref)
    depth = x_s.shape[1] // CHUNKS
    copies = []
    for c in range(CHUNKS):
        part = pl.ds(c * depth, depth)
        copies.append(bring([
            (wk_ref.at[part, :], w_s.at[part, pl.ds(0, HD)]),
            (wv_ref.at[part, :], w_s.at[part, pl.ds(HD, HD)]),
            (wq_ref.at[part, :], w_s.at[part, pl.ds(2 * HD, 2 * HD)]),
            (x_ref.at[:, part], x_s.at[:, part]),
        ], sems, 4 * c))
    copies.append(bring([(big_ref, big_s), (small_ref, small_s)], sems, 4 * CHUNKS))
    y = jnp.zeros((2 * SPAN, 4 * HD), F32)
    for c in range(CHUNKS):
        for copy in copies[c]:
            copy.wait()
        part = slice(c * depth, (c + 1) * depth)
        y = y + jnp.dot(x_s[:, part], w_s[part, :], preferred_element_type=F32)
    for copy in copies[CHUNKS]:
        copy.wait()
    scale = HD ** (-0.5) * math.log2(math.e)

    for s in range(2):
        qs = s ^ slot
        here = jnp.where(qs == 0, span, SPANS - 1 - span)
        rows = slice(s * SPAN, (s + 1) * SPAN)
        to = pl.multiple_of(qs * 2 * SPAN, 2 * SPAN)
        kv_ref[pl.ds(to, SPAN), :] = rotated(y[rows, :HD], here, big_s, small_s).astype(BF16)
        for c in range(SPAN // HD):
            tile = y[s * SPAN + c * HD:s * SPAN + (c + 1) * HD, HD:2 * HD]
            kv_ref[pl.ds(to + SPAN + c * HD, HD), :] = tile.T.astype(BF16)
        for h in range(2):
            r = rotated(y[rows, (2 + h) * HD:(3 + h) * HD], here, big_s, small_s) * scale
            q_ref[qs, :, h * SPAN:(h + 1) * SPAN] = r.T.astype(BF16)


def project(order, states, w_key, w_value, w_query, tables):
    rows, width = states.shape
    return pl.pallas_call(
        project_kernel,
        in_specs=[SCALAR] + [HBM] * 6,
        out_specs=[LOCAL] * 2,
        out_shape=[
            jax.ShapeDtypeStruct((4 * SPAN, HD), BF16),
            jax.ShapeDtypeStruct((2, HD, 2 * SPAN), BF16),
        ],
        scratch_shapes=[
            pltpu.VMEM((rows, width), BF16),
            pltpu.VMEM((width, 4 * HD), BF16),
            *[pltpu.VMEM(t.shape, F32) for t in tables],
            pltpu.SemaphoreType.DMA((4 * CHUNKS + 2,)),
        ],
        compiler_params=WIDE,
        cost_estimate=pl.CostEstimate(flops=rows * width * 8 * HD, bytes_accessed=13 * 2**20, transcendentals=0),
    )(order, states, w_key, w_value, w_query, *tables)


def attn_kernel(many, units, asked, begins, ends, order_ref, start_ref, *refs):
    n = len(units)
    kv = refs[:many]
    q_ref = refs[many]
    at = many + 1
    before = {}
    for qs in asked:
        if qs not in begins:
            before[qs] = refs[at:at + 2]
            at += 2
    outs = {}
    for qs in asked:
        wide = 1 if qs in ends else 2
        outs[qs] = refs[at:at + wide]
        at += wide
    kb, vb, m_ref, acc_ref, span_ref, sems = refs[at:]
    me = lax.axis_index("ctx")
    x0, z0, c0 = me // 8, (me // 2) % 4, me % 2
    own = own_spans(order_ref)[1]

    for t, (src, base, where, late, _) in enumerate(units):
        pltpu.make_async_copy(kv[src].at[pl.ds(base, SPAN), :], kb.at[t], sems.at[t, 0]).start()
        for c in range(4):
            pltpu.make_async_copy(
                kv[src].at[pl.ds(base + SPAN + c * HD, HD), :],
                vb.at[t, pl.ds(0, HD), pl.ds(c * HD, HD)],
                sems.at[t, 1 + c],
            ).start()
        if isinstance(where, tuple):
            dx, dz, dc = where
            who = ((x0 ^ dx) * 4 + ((z0 + dz + 4) % 4)) * 2 + (c0 ^ dc)
        else:
            who = where
        early = jnp.minimum(order_ref[2 * who], order_ref[2 * who + 1])
        span = SPANS - 1 - early if late else early
        if not isinstance(where, tuple):
            span = jnp.where(me == who, SPANS, span)
        span_ref[t] = span
    vb[:, HD:, :] = jnp.ones((n, 16, SPAN), BF16)
    for qs in asked:
        if qs in begins:
            m_ref[qs] = jnp.full(m_ref.shape[1:], neg_large, F32)
            acc_ref[qs] = jnp.zeros(acc_ref.shape[1:], F32)
        else:
            m_ref[qs] = before[qs][0][...]
            acc_ref[qs] = before[qs][1][...]

    def first_of(p):
        low = jnp.int32(0)
        for d in range(3):
            s = start_ref[d]
            low = jnp.where(s <= p, s, low)
        return low

    def block(u, qs, masked):
        k = kb[u]
        v = vb[u]
        qspan = SPANS - 1 - own if qs else own
        wide = 256
        parts = [slice(c * wide, (c + 1) * wide) for c in range(2 * SPAN // wide)]
        scores = [jnp.dot(k, q_ref[qs, :, sl], preferred_element_type=F32) for sl in parts]
        weights, factors = [], []
        for s, sl in zip(scores, parts):
            if masked:
                qpos = lax.broadcasted_iota(jnp.int32, (1, wide), 1) + (sl.start % SPAN + qspan * SPAN)
                low = first_of(qpos)
                kpos = lax.broadcasted_iota(jnp.int32, (SPAN, 1), 0) + span_ref[u] * SPAN
                s = jnp.where((kpos <= qpos) & (kpos >= low), s, neg_large)
            old = m_ref[qs, :, sl]
            new = jnp.maximum(old, jnp.max(s, 0, keepdims=True))
            weights.append(jnp.exp2(s - new).astype(BF16))
            factors.append(jnp.exp2(old - new))
            m_ref[qs, :, sl] = new
        for p, f, sl in zip(weights, factors, parts):
            acc_ref[qs, :, sl] = acc_ref[qs, :, sl] * f + jnp.dot(v, p, preferred_element_type=F32)

    def visit(u, qs):
        qspan = SPANS - 1 - own if qs else own
        kspan = span_ref[u]
        low_first = first_of(qspan * SPAN)
        low_last = first_of(qspan * SPAN + SPAN - 1)
        seen = (kspan <= qspan) & (kspan * SPAN + SPAN - 1 >= low_first)
        cut = (kspan == qspan) | (kspan * SPAN < low_last)

        @pl.when(seen & cut)
        def _():
            block(u, qs, True)

        @pl.when(seen & jnp.logical_not(cut))
        def _():
            block(u, qs, False)

    def steps(first, last, who):
        def step(u, carry):
            pltpu.make_async_copy(kb.at[u], kb.at[u], sems.at[u, 0]).wait()
            for c in range(4):
                spot = vb.at[u, pl.ds(0, HD), pl.ds(c * HD, HD)]
                pltpu.make_async_copy(spot, spot, sems.at[u, 1 + c]).wait()
            for qs in who:
                visit(u, qs)
            return carry

        lax.fori_loop(first, last, step, 0)

    t = 0
    while t < n:
        e = t
        while e < n and units[e][4] == units[t][4]:
            e += 1
        steps(t, e, units[t][4])
        t = e

    for qs in asked:
        if qs in ends:
            for h in range(2):
                sl = slice(h * SPAN, (h + 1) * SPAN)
                value = acc_ref[qs, 0:HD, sl] / acc_ref[qs, HD:HD + 1, sl]
                outs[qs][0][:, h * HD:(h + 1) * HD] = value.T.astype(BF16)
        else:
            outs[qs][0][...] = m_ref[qs]
            outs[qs][1][...] = acc_ref[qs]


def attend(order, starts, arrays, units, q, states, ends=()):
    n = len(units)
    many = len(arrays)
    asked = tuple(sorted(states))
    begins = tuple(s for s in asked if states[s] is None)
    inner = []
    shapes = []
    for s in asked:
        if s not in begins:
            inner += list(states[s])
        if s in ends:
            shapes.append(jax.ShapeDtypeStruct((SPAN, 2 * HD), BF16))
        else:
            shapes.append(jax.ShapeDtypeStruct((1, 2 * SPAN), F32))
            shapes.append(jax.ShapeDtypeStruct((HD + 16, 2 * SPAN), F32))
    work = sum(len(u[4]) for u in units)
    got = pl.pallas_call(
        functools.partial(attn_kernel, many, units, asked, begins, ends),
        in_specs=[SCALAR, SCALAR] + [ANYWHERE] * many + [LOCAL] * (1 + len(inner)),
        out_specs=[LOCAL] * len(shapes),
        out_shape=shapes,
        scratch_shapes=[
            pltpu.VMEM((n, SPAN, HD), BF16),
            pltpu.VMEM((n, HD + 16, SPAN), BF16),
            pltpu.VMEM((2, 1, 2 * SPAN), F32),
            pltpu.VMEM((2, HD + 16, 2 * SPAN), F32),
            pltpu.SMEM((n,), jnp.int32),
            pltpu.SemaphoreType.DMA((n, 5)),
        ],
        compiler_params=LIMIT,
        cost_estimate=pl.CostEstimate(
            flops=work * 10**6, bytes_accessed=n * 2**10, transcendentals=work * 2**10
        ),
    )(order, starts, *arrays, q, *inner)
    out = {}
    at = 0
    for s in asked:
        if s in ends:
            out[s] = got[at]
            at += 1
        else:
            out[s] = (got[at], got[at + 1])
            at += 2
    return out


def out_kernel(first, *refs):
    parts, w_ref, straight, crossed, out_ref, w_s, sems = refs[0:4], refs[4], refs[5:8], refs[8:11], *refs[11:]
    head = lax.axis_index("head").astype(jnp.int32)
    core = lax.axis_index("ctx") % 2
    cols = out_ref.shape[1]
    block = head + 1 - 2 * (head % 2) if first else head
    at = pl.multiple_of(block * cols, cols)
    own = pltpu.make_async_copy(w_ref.at[:, pl.ds(at, cols)], w_s.at[0], sems.at[0])
    own.start()

    def fetch(source):
        for t in range(3):
            pltpu.make_async_copy(source[t], w_s.at[1 + t], sems.at[1 + t]).start()

    use_straight = core == (1 if first else 0)

    @pl.when(use_straight)
    def _():
        fetch(straight)

    @pl.when(jnp.logical_not(use_straight))
    def _():
        fetch(crossed)

    total = None
    for t in range(4):
        pltpu.make_async_copy(w_s.at[t], w_s.at[t], sems.at[t]).wait()
        part = jnp.dot(parts[t][...], w_s[t], preferred_element_type=F32)
        total = part if total is None else total + part
    out_ref[...] = total.astype(out_ref.dtype)


def output(parts, straight, crossed, w_out, first):
    cols = w_out.shape[1] // 8
    return pl.pallas_call(
        functools.partial(out_kernel, first),
        in_specs=[LOCAL] * 4 + [ANYWHERE] * 7,
        out_specs=LOCAL,
        out_shape=jax.ShapeDtypeStruct((SPAN, cols), BF16 if first else F32),
        scratch_shapes=[pltpu.VMEM((4, 2 * HD, cols), BF16), pltpu.SemaphoreType.DMA((4,))],
        compiler_params=LIMIT,
        cost_estimate=pl.CostEstimate(flops=SPAN * 1024 * cols * 2, bytes_accessed=3 * 2**20, transcendentals=0),
    )(*parts, w_out, *straight, *crossed)


def join_kernel(order_ref, own0, other0, own1, other1, out_ref):
    slot = own_spans(order_ref)[0]
    for qs, (own, other) in enumerate(((own0, other0), (own1, other1))):
        row = pl.multiple_of((slot ^ qs) * SPAN, SPAN)
        out_ref[pl.ds(row, SPAN), :] = (own[...] + other[...].astype(F32)).astype(BF16)


def join(order, own, other):
    cols = own[0].shape[1]
    return pl.pallas_call(
        join_kernel,
        in_specs=[SCALAR] + [LOCAL] * 4,
        out_specs=LOCAL,
        out_shape=jax.ShapeDtypeStruct((2 * SPAN, cols), BF16),
        compiler_params=LIMIT,
        cost_estimate=pl.CostEstimate(flops=2 * SPAN * cols, bytes_accessed=4 * 2**20, transcendentals=0),
    )(order, own[0], other[0], own[1], other[1])


def pairs(move):
    def flat(x, y, z, c):
        x, y, z, c = x % 4, y % 4, z % 4, c % 2
        return ((x % 2 * 4 + z) * 2 + c) * 8 + y * 2 + x // 2

    return [
        (flat(x, y, z, c), flat(*move(x, y, z, c)))
        for x in range(4) for y in range(4) for z in range(4) for c in range(2)
    ]


to_pair = pairs(lambda x, y, z, c: (x ^ 1, y, z, c))
to_far = pairs(lambda x, y, z, c: (x + 2, y, z, c))
to_core = pairs(lambda x, y, z, c: (x, y, z, c + 1))
z_up = pairs(lambda x, y, z, c: (x, y, z + 1, c))
z_down = pairs(lambda x, y, z, c: (x, y, z - 1, c))
y_up = pairs(lambda x, y, z, c: (x, y + 1, z, c))
y_down = pairs(lambda x, y, z, c: (x, y - 1, z, c))
y_two = pairs(lambda x, y, z, c: (x, y + 2, z, c))


def send(value, to):
    return lax.ppermute(value, ("ctx", "head"), to)


def after(values, *others):
    return lax.optimization_barrier((values, others))[0]


def per_device(states, seg_ids, span_order, w_query, w_key, w_value, w_out):
    head = lax.axis_index("head").astype(jnp.int32)
    core = lax.axis_index("ctx").astype(jnp.int32) % 2
    y, far = head // 2, head % 2
    starts = jnp.sum(seg_ids[None, :] < jnp.arange(1, 4, dtype=jnp.int32)[:, None], 1, dtype=jnp.int32)
    tables = tuple(jnp.asarray(t) for t in rope_tables())

    rels = {
        "own": (0, 0), "pair": (1, 0), "below": (0, -1), "above": (0, 1),
        "pair_below": (1, -1), "pair_above": (1, 1), "two": (0, 2), "far": (1, 2),
    }
    held = {}

    def hold(name, crossed, array):
        for late in (0, 1):
            held[name, late, crossed] = (array, late * 2 * SPAN)

    def across_cores(names, *others):
        values = tuple(held[name, 0, 0][0] for name in names)
        for name, value in zip(names, after(values, *others) if others else values):
            hold(name, 1, send(value, to_core))

    def stage(picks, state, ends=()):
        arrays, units, index = [], [], {}
        for names, late, who in picks:
            for name in names:
                for c in (0, 1):
                    array, row = held[name, late, c]
                    if id(array) not in index:
                        index[id(array)] = len(arrays)
                        arrays.append(array)
                    units.append((index[id(array)], row, (*rels[name], c), late, who))
        return attend(span_order, starts, arrays, tuple(units), q, state, ends)

    own, q = project(span_order, states, w_key, w_value, w_query, tables)
    hold("own", 0, own)
    below, above, pair = send(own, z_up), send(own, z_down), send(own, to_pair)
    across_cores(("own",))

    half = w_out.shape[1] // 8

    def columns(step):
        block = 2 * ((y + step) % 4) + (far ^ core)
        return lax.dynamic_slice_in_dim(w_out, block * half, half, 1)

    straight = [send(columns(1), y_up), send(columns(3), y_down), send(columns(2), y_two)]
    both, ql, qe = (0, 1), (1,), (0,)
    s = stage([(("own",), 0, both), (("own",), 1, ql)], {0: None, 1: None})
    below, pair, above, straight = after((below, pair, above, straight), s)
    hold("below", 0, below)
    hold("above", 0, above)
    hold("pair", 0, pair)
    two = send(below, z_up)
    pair_above = send(pair, z_down)
    pair_below = send(below, to_pair)
    near = ("below", "above", "pair")
    across_cores(near)
    crossed = [send(w, to_core) for w in straight]
    s = stage([(near, 0, both), (near, 1, ql)], s)
    two, pair_above, pair_below = after((two, pair_above, pair_below), s)
    hold("two", 0, two)
    hold("pair_above", 0, pair_above)
    hold("pair_below", 0, pair_below)
    far_early = send(pair_below[:2 * SPAN], z_up)
    far_late = send(pair_above[2 * SPAN:], z_down)
    rest = ("two", "pair_above", "pair_below")
    across_cores(rest)
    s = stage([(rest, 0, both)], s)
    far_early = after(far_early, s)
    held["far", 0, 0] = (far_early, 0)
    held["far", 0, 1] = (send(far_early, to_core), 0)
    early = stage([(("far",), 0, qe)], {0: s[0]}, qe)[0]
    early_up, early_down = send(early, y_up), send(early, y_down)
    s = stage([(("far",), 0, ql), (rest, 1, ql)], {1: after(s[1], early)})
    far_late, early_up = after((far_late, early_up), s)
    early_across = send(early_up, y_up)
    held["far", 1, 0] = (far_late, 0)
    held["far", 1, 1] = (send(far_late, to_core), 0)
    late = stage([(("far",), 1, ql)], s, ql)[1]
    late_up, late_down = send(late, y_up), send(late, y_down)

    early_parts = [early, early_up, early_down, early_across]
    early_theirs = output(after(early_parts, late), straight, crossed, w_out, True)
    early_other = send(early_theirs, to_far)
    late_up, late_down = after((late_up, late_down), early_theirs)
    late_parts = [late, late_up, late_down, send(late_down, y_down)]
    late_theirs = output(late_parts, straight, crossed, w_out, True)
    late_other = send(late_theirs, to_far)
    early_own = output(after(early_parts, early_theirs), straight, crossed, w_out, False)
    late_own = output(after(late_parts, late_theirs), straight, crossed, w_out, False)
    return join(span_order, [early_own, late_own], [early_other, late_other])


def solution(mesh):
    in_specs = (
        P("ctx", None),
        P(),
        P(),
        P(None, "head"),
        P(None, "head"),
        P(None, "head"),
        P("head", None),
    )
    out_specs = P("ctx", "head")
    return jax.shard_map(
        per_device, mesh=mesh, in_specs=in_specs, out_specs=out_specs, check_vma=False
    )
```

```python
import functools
import math

import jax
import jax.numpy as jnp
import numpy as np
from jax import lax
from jax.experimental import pallas as pl
from jax.experimental.pallas import tpu as pltpu
from jax.sharding import PartitionSpec as P

HD = 128
SPAN = 512
SPANS = 32
CHUNKS = 4
rope_base = 500000.0
neg_large = -1e30
F32 = jnp.float32
BF16 = jnp.bfloat16
HBM = pl.BlockSpec(memory_space=pltpu.HBM)
ANYWHERE = pl.BlockSpec(memory_space=pl.ANY)
SCALAR = pl.BlockSpec(memory_space=pltpu.SMEM)
LOCAL = pl.BlockSpec(memory_space=pltpu.VMEM)
LIMIT = pltpu.CompilerParams(vmem_limit_bytes=20 * 2**20)
WIDE = pltpu.CompilerParams(vmem_limit_bytes=57 * 2**20)


def rope_tables():
    freq = rope_base ** (-np.arange(64, dtype=np.float64) * 2.0 / HD)
    sign = np.concatenate([-np.ones(64), np.ones(64)])

    def pair(pos):
        ang = np.concatenate([pos[:, None] * freq, pos[:, None] * freq], 1)
        return np.stack([np.cos(ang), np.sin(ang) * sign]).astype(np.float32)

    return pair(np.arange(SPANS) * float(SPAN)), pair(np.arange(SPAN) * 1.0)


def rotated(x, span, big_ref, small_ref):
    cb = big_ref[0, pl.ds(span, 1), :]
    sb = big_ref[1, pl.ds(span, 1), :]
    cs = small_ref[0]
    ss = small_ref[1]
    cos = cb * cs - sb * ss
    sin = sb * cs + cb * ss
    return x * cos + pltpu.roll(x, 64, 1) * sin


def own_spans(order_ref):
    me = lax.axis_index("ctx")
    a, b = order_ref[2 * me], order_ref[2 * me + 1]
    return jnp.where(a < b, 0, 1).astype(jnp.int32), jnp.minimum(a, b)


def bring(pairs_of_refs, sems, base):
    copies = [pltpu.make_async_copy(a, b, sems.at[base + t]) for t, (a, b) in enumerate(pairs_of_refs)]
    for copy in copies:
        copy.start()
    return copies


def project_kernel(
    order_ref, x_ref, wk_ref, wv_ref, wq_ref, big_ref, small_ref,
    kv_ref, q_ref, x_s, w_s, big_s, small_s, sems,
):
    slot, span = own_spans(order_ref)
    depth = x_s.shape[1] // CHUNKS
    copies = []
    for c in range(CHUNKS):
        part = pl.ds(c * depth, depth)
        copies.append(bring([
            (wk_ref.at[part, :], w_s.at[part, pl.ds(0, HD)]),
            (wv_ref.at[part, :], w_s.at[part, pl.ds(HD, HD)]),
            (wq_ref.at[part, :], w_s.at[part, pl.ds(2 * HD, 2 * HD)]),
            (x_ref.at[:, part], x_s.at[:, part]),
        ], sems, 4 * c))
    copies.append(bring([(big_ref, big_s), (small_ref, small_s)], sems, 4 * CHUNKS))
    y = jnp.zeros((2 * SPAN, 4 * HD), F32)
    for c in range(CHUNKS):
        for copy in copies[c]:
            copy.wait()
        part = slice(c * depth, (c + 1) * depth)
        y = y + jnp.dot(x_s[:, part], w_s[part, :], preferred_element_type=F32)
    for copy in copies[CHUNKS]:
        copy.wait()
    scale = HD ** (-0.5) * math.log2(math.e)

    for s in range(2):
        qs = s ^ slot
        here = jnp.where(qs == 0, span, SPANS - 1 - span)
        rows = slice(s * SPAN, (s + 1) * SPAN)
        to = pl.multiple_of(qs * 2 * SPAN, 2 * SPAN)
        kv_ref[pl.ds(to, SPAN), :] = rotated(y[rows, :HD], here, big_s, small_s).astype(BF16)
        for c in range(SPAN // HD):
            tile = y[s * SPAN + c * HD:s * SPAN + (c + 1) * HD, HD:2 * HD]
            kv_ref[pl.ds(to + SPAN + c * HD, HD), :] = tile.T.astype(BF16)
        for h in range(2):
            r = rotated(y[rows, (2 + h) * HD:(3 + h) * HD], here, big_s, small_s) * scale
            q_ref[qs, :, h * SPAN:(h + 1) * SPAN] = r.T.astype(BF16)


def project(order, states, w_key, w_value, w_query, tables):
    rows, width = states.shape
    return pl.pallas_call(
        project_kernel,
        in_specs=[SCALAR] + [HBM] * 6,
        out_specs=[LOCAL] * 2,
        out_shape=[
            jax.ShapeDtypeStruct((4 * SPAN, HD), BF16),
            jax.ShapeDtypeStruct((2, HD, 2 * SPAN), BF16),
        ],
        scratch_shapes=[
            pltpu.VMEM((rows, width), BF16),
            pltpu.VMEM((width, 4 * HD), BF16),
            *[pltpu.VMEM(t.shape, F32) for t in tables],
            pltpu.SemaphoreType.DMA((4 * CHUNKS + 2,)),
        ],
        compiler_params=WIDE,
        cost_estimate=pl.CostEstimate(flops=rows * width * 8 * HD, bytes_accessed=13 * 2**20, transcendentals=0),
    )(order, states, w_key, w_value, w_query, *tables)


def attn_kernel(many, units, asked, begins, ends, order_ref, start_ref, *refs):
    n = len(units)
    kv = refs[:many]
    q_ref = refs[many]
    at = many + 1
    before = {}
    for qs in asked:
        if qs not in begins:
            before[qs] = refs[at:at + 2]
            at += 2
    outs = {}
    for qs in asked:
        wide = 1 if qs in ends else 2
        outs[qs] = refs[at:at + wide]
        at += wide
    kb, vb, m_ref, acc_ref, span_ref, sems = refs[at:]
    me = lax.axis_index("ctx")
    x0, z0, c0 = me // 8, (me // 2) % 4, me % 2
    own = own_spans(order_ref)[1]

    for t, (src, base, where, late, _) in enumerate(units):
        pltpu.make_async_copy(kv[src].at[pl.ds(base, SPAN), :], kb.at[t], sems.at[t, 0]).start()
        for c in range(4):
            pltpu.make_async_copy(
                kv[src].at[pl.ds(base + SPAN + c * HD, HD), :],
                vb.at[t, pl.ds(0, HD), pl.ds(c * HD, HD)],
                sems.at[t, 1 + c],
            ).start()
        if isinstance(where, tuple):
            dx, dz, dc = where
            who = ((x0 ^ dx) * 4 + ((z0 + dz + 4) % 4)) * 2 + (c0 ^ dc)
        else:
            who = where
        early = jnp.minimum(order_ref[2 * who], order_ref[2 * who + 1])
        span = SPANS - 1 - early if late else early
        if not isinstance(where, tuple):
            span = jnp.where(me == who, SPANS, span)
        span_ref[t] = span
    vb[:, HD:, :] = jnp.ones((n, 16, SPAN), BF16)
    for qs in asked:
        if qs in begins:
            m_ref[qs] = jnp.full(m_ref.shape[1:], neg_large, F32)
            acc_ref[qs] = jnp.zeros(acc_ref.shape[1:], F32)
        else:
            m_ref[qs] = before[qs][0][...]
            acc_ref[qs] = before[qs][1][...]

    def first_of(p):
        low = jnp.int32(0)
        for d in range(3):
            s = start_ref[d]
            low = jnp.where(s <= p, s, low)
        return low

    def block(u, qs, masked):
        k = kb[u]
        v = vb[u]
        qspan = SPANS - 1 - own if qs else own
        wide = 256
        parts = [slice(c * wide, (c + 1) * wide) for c in range(2 * SPAN // wide)]
        scores = [jnp.dot(k, q_ref[qs, :, sl], preferred_element_type=F32) for sl in parts]
        weights, factors = [], []
        for s, sl in zip(scores, parts):
            if masked:
                qpos = lax.broadcasted_iota(jnp.int32, (1, wide), 1) + (sl.start % SPAN + qspan * SPAN)
                low = first_of(qpos)
                kpos = lax.broadcasted_iota(jnp.int32, (SPAN, 1), 0) + span_ref[u] * SPAN
                s = jnp.where((kpos <= qpos) & (kpos >= low), s, neg_large)
            old = m_ref[qs, :, sl]
            new = jnp.maximum(old, jnp.max(s, 0, keepdims=True))
            weights.append(jnp.exp2(s - new).astype(BF16))
            factors.append(jnp.exp2(old - new))
            m_ref[qs, :, sl] = new
        for p, f, sl in zip(weights, factors, parts):
            acc_ref[qs, :, sl] = acc_ref[qs, :, sl] * f + jnp.dot(v, p, preferred_element_type=F32)

    def visit(u, qs):
        qspan = SPANS - 1 - own if qs else own
        kspan = span_ref[u]
        low_first = first_of(qspan * SPAN)
        low_last = first_of(qspan * SPAN + SPAN - 1)
        seen = (kspan <= qspan) & (kspan * SPAN + SPAN - 1 >= low_first)
        cut = (kspan == qspan) | (kspan * SPAN < low_last)

        @pl.when(seen & cut)
        def _():
            block(u, qs, True)

        @pl.when(seen & jnp.logical_not(cut))
        def _():
            block(u, qs, False)

    def steps(first, last, who):
        def step(u, carry):
            pltpu.make_async_copy(kb.at[u], kb.at[u], sems.at[u, 0]).wait()
            for c in range(4):
                spot = vb.at[u, pl.ds(0, HD), pl.ds(c * HD, HD)]
                pltpu.make_async_copy(spot, spot, sems.at[u, 1 + c]).wait()
            for qs in who:
                visit(u, qs)
            return carry

        lax.fori_loop(first, last, step, 0)

    t = 0
    while t < n:
        e = t
        while e < n and units[e][4] == units[t][4]:
            e += 1
        steps(t, e, units[t][4])
        t = e

    for qs in asked:
        if qs in ends:
            for h in range(2):
                sl = slice(h * SPAN, (h + 1) * SPAN)
                value = acc_ref[qs, 0:HD, sl] / acc_ref[qs, HD:HD + 1, sl]
                outs[qs][0][:, h * HD:(h + 1) * HD] = value.T.astype(BF16)
        else:
            outs[qs][0][...] = m_ref[qs]
            outs[qs][1][...] = acc_ref[qs]


def attend(order, starts, arrays, units, q, states, ends=()):
    n = len(units)
    many = len(arrays)
    asked = tuple(sorted(states))
    begins = tuple(s for s in asked if states[s] is None)
    inner = []
    shapes = []
    for s in asked:
        if s not in begins:
            inner += list(states[s])
        if s in ends:
            shapes.append(jax.ShapeDtypeStruct((SPAN, 2 * HD), BF16))
        else:
            shapes.append(jax.ShapeDtypeStruct((1, 2 * SPAN), F32))
            shapes.append(jax.ShapeDtypeStruct((HD + 16, 2 * SPAN), F32))
    work = sum(len(u[4]) for u in units)
    got = pl.pallas_call(
        functools.partial(attn_kernel, many, units, asked, begins, ends),
        in_specs=[SCALAR, SCALAR] + [ANYWHERE] * many + [LOCAL] * (1 + len(inner)),
        out_specs=[LOCAL] * len(shapes),
        out_shape=shapes,
        scratch_shapes=[
            pltpu.VMEM((n, SPAN, HD), BF16),
            pltpu.VMEM((n, HD + 16, SPAN), BF16),
            pltpu.VMEM((2, 1, 2 * SPAN), F32),
            pltpu.VMEM((2, HD + 16, 2 * SPAN), F32),
            pltpu.SMEM((n,), jnp.int32),
            pltpu.SemaphoreType.DMA((n, 5)),
        ],
        compiler_params=LIMIT,
        cost_estimate=pl.CostEstimate(
            flops=work * 10**6, bytes_accessed=n * 2**10, transcendentals=work * 2**10
        ),
    )(order, starts, *arrays, q, *inner)
    out = {}
    at = 0
    for s in asked:
        if s in ends:
            out[s] = got[at]
            at += 1
        else:
            out[s] = (got[at], got[at + 1])
            at += 2
    return out


def out_kernel(first, *refs):
    parts, w_ref, straight, crossed, out_ref, w_s, sems = refs[0:4], refs[4], refs[5:8], refs[8:11], *refs[11:]
    head = lax.axis_index("head").astype(jnp.int32)
    core = lax.axis_index("ctx") % 2
    cols = out_ref.shape[1]
    block = head + 1 - 2 * (head % 2) if first else head
    at = pl.multiple_of(block * cols, cols)
    own = pltpu.make_async_copy(w_ref.at[:, pl.ds(at, cols)], w_s.at[0], sems.at[0])
    own.start()

    def fetch(source):
        for t in range(3):
            pltpu.make_async_copy(source[t], w_s.at[1 + t], sems.at[1 + t]).start()

    use_straight = core == (1 if first else 0)

    @pl.when(use_straight)
    def _():
        fetch(straight)

    @pl.when(jnp.logical_not(use_straight))
    def _():
        fetch(crossed)

    total = None
    for t in range(4):
        pltpu.make_async_copy(w_s.at[t], w_s.at[t], sems.at[t]).wait()
        part = jnp.dot(parts[t][...], w_s[t], preferred_element_type=F32)
        total = part if total is None else total + part
    out_ref[...] = total.astype(out_ref.dtype)


def output(parts, straight, crossed, w_out, first):
    cols = w_out.shape[1] // 8
    return pl.pallas_call(
        functools.partial(out_kernel, first),
        in_specs=[LOCAL] * 4 + [ANYWHERE] * 7,
        out_specs=LOCAL,
        out_shape=jax.ShapeDtypeStruct((SPAN, cols), BF16 if first else F32),
        scratch_shapes=[pltpu.VMEM((4, 2 * HD, cols), BF16), pltpu.SemaphoreType.DMA((4,))],
        compiler_params=LIMIT,
        cost_estimate=pl.CostEstimate(flops=2**10, bytes_accessed=2**10, transcendentals=0),
    )(*parts, w_out, *straight, *crossed)


def join_kernel(order_ref, own0, other0, own1, other1, out_ref):
    slot = own_spans(order_ref)[0]
    for qs, (own, other) in enumerate(((own0, other0), (own1, other1))):
        row = pl.multiple_of((slot ^ qs) * SPAN, SPAN)
        out_ref[pl.ds(row, SPAN), :] = (own[...] + other[...].astype(F32)).astype(BF16)


def join(order, own, other):
    cols = own[0].shape[1]
    return pl.pallas_call(
        join_kernel,
        in_specs=[SCALAR] + [LOCAL] * 4,
        out_specs=LOCAL,
        out_shape=jax.ShapeDtypeStruct((2 * SPAN, cols), BF16),
        compiler_params=LIMIT,
        cost_estimate=pl.CostEstimate(flops=2 * SPAN * cols, bytes_accessed=4 * 2**20, transcendentals=0),
    )(order, own[0], other[0], own[1], other[1])


def pairs(move):
    def flat(x, y, z, c):
        x, y, z, c = x % 4, y % 4, z % 4, c % 2
        return ((x % 2 * 4 + z) * 2 + c) * 8 + y * 2 + x // 2

    return [
        (flat(x, y, z, c), flat(*move(x, y, z, c)))
        for x in range(4) for y in range(4) for z in range(4) for c in range(2)
    ]


to_pair = pairs(lambda x, y, z, c: (x ^ 1, y, z, c))
to_far = pairs(lambda x, y, z, c: (x + 2, y, z, c))
to_core = pairs(lambda x, y, z, c: (x, y, z, c + 1))
z_up = pairs(lambda x, y, z, c: (x, y, z + 1, c))
z_down = pairs(lambda x, y, z, c: (x, y, z - 1, c))
y_up = pairs(lambda x, y, z, c: (x, y + 1, z, c))
y_down = pairs(lambda x, y, z, c: (x, y - 1, z, c))
y_two = pairs(lambda x, y, z, c: (x, y + 2, z, c))


def send(value, to):
    return lax.ppermute(value, ("ctx", "head"), to)


def after(values, *others):
    return lax.optimization_barrier((values, others))[0]


def per_device(states, seg_ids, span_order, w_query, w_key, w_value, w_out):
    head = lax.axis_index("head").astype(jnp.int32)
    core = lax.axis_index("ctx").astype(jnp.int32) % 2
    y, far = head // 2, head % 2
    starts = jnp.sum(seg_ids[None, :] < jnp.arange(1, 4, dtype=jnp.int32)[:, None], 1, dtype=jnp.int32)
    tables = tuple(jnp.asarray(t) for t in rope_tables())

    rels = {
        "own": (0, 0), "pair": (1, 0), "below": (0, -1), "above": (0, 1),
        "pair_below": (1, -1), "pair_above": (1, 1), "two": (0, 2), "far": (1, 2),
    }
    held = {}

    def hold(name, crossed, array):
        for late in (0, 1):
            held[name, late, crossed] = (array, late * 2 * SPAN)

    def across_cores(names, *others):
        values = tuple(held[name, 0, 0][0] for name in names)
        for name, value in zip(names, after(values, *others) if others else values):
            hold(name, 1, send(value, to_core))

    def stage(picks, state, ends=()):
        arrays, units, index = [], [], {}
        for names, late, who in picks:
            for name in names:
                for c in (0, 1):
                    array, row = held[name, late, c]
                    if id(array) not in index:
                        index[id(array)] = len(arrays)
                        arrays.append(array)
                    units.append((index[id(array)], row, (*rels[name], c), late, who))
        return attend(span_order, starts, arrays, tuple(units), q, state, ends)

    own, q = project(span_order, states, w_key, w_value, w_query, tables)
    hold("own", 0, own)
    below, above, pair = send(own, z_up), send(own, z_down), send(own, to_pair)
    across_cores(("own",))

    half = w_out.shape[1] // 8

    def columns(step):
        block = 2 * ((y + step) % 4) + (far ^ core)
        return lax.dynamic_slice_in_dim(w_out, block * half, half, 1)

    straight = [send(columns(1), y_up), send(columns(3), y_down), send(columns(2), y_two)]
    both, ql, qe = (0, 1), (1,), (0,)
    s = stage([(("own",), 0, both), (("own",), 1, ql)], {0: None, 1: None})
    below, pair, above, straight = after((below, pair, above, straight), s)
    hold("below", 0, below)
    hold("above", 0, above)
    hold("pair", 0, pair)
    two = send(below, z_up)
    pair_above = send(pair, z_down)
    pair_below = send(below, to_pair)
    near = ("below", "above", "pair")
    across_cores(near)
    s = stage([(near, 0, both), (near, 1, ql)], s)
    two, pair_above, pair_below = after((two, pair_above, pair_below), s)
    hold("two", 0, two)
    hold("pair_above", 0, pair_above)
    hold("pair_below", 0, pair_below)
    far_early = send(pair_below[:2 * SPAN], z_up)
    far_late = send(pair_above[2 * SPAN:], z_down)
    rest = ("two", "pair_above", "pair_below")
    across_cores(rest)
    s = stage([(rest, 0, both)], s)
    far_early, far_late, straight = after((far_early, far_late, straight), s)
    for late, array in ((0, far_early), (1, far_late)):
        held["far", late, 0] = (array, 0)
        held["far", late, 1] = (send(array, to_core), 0)
    crossed = [send(w, to_core) for w in straight]
    early = stage([(("far",), 0, qe)], {0: after(s[0], far_late)}, qe)[0]
    early_moved = [send(early, y_up), send(early, y_down), send(early, y_two)]
    late = stage(
        [(("far",), 0, ql), (rest, 1, ql), (("far",), 1, ql)], {1: after(s[1], early, crossed)}, ql
    )[1]
    late_moved = [send(late, y_up), send(late, y_down), send(late, y_two)]

    early_parts = [early, *after(early_moved, late)]
    early_theirs = output(early_parts, straight, crossed, w_out, True)
    early_other = send(early_theirs, to_far)
    late_parts = [late, *after(late_moved, early_theirs)]
    late_theirs = output(late_parts, straight, crossed, w_out, True)
    late_other = send(late_theirs, to_far)
    early_own = output(after(early_parts, late_theirs, early_other), straight, crossed, w_out, False)
    late_own = output(after(late_parts, late_theirs, early_other), straight, crossed, w_out, False)
    return join(span_order, [early_own, late_own], [early_other, late_other])


def solution(mesh):
    in_specs = (
        P("ctx", None),
        P(),
        P(),
        P(None, "head"),
        P(None, "head"),
        P(None, "head"),
        P("head", None),
    )
    out_specs = P("ctx", "head")
    return jax.shard_map(
        per_device, mesh=mesh, in_specs=in_specs, out_specs=out_specs, check_vma=False
    )
```

```python
import functools
import math

import jax
import jax.numpy as jnp
import numpy as np
from jax import lax
from jax.experimental import pallas as pl
from jax.experimental.pallas import tpu as pltpu
from jax.sharding import PartitionSpec as P

HD = 128
SPAN = 512
SPANS = 32
CHUNKS = 8
rope_base = 500000.0
neg_large = -1e30
F32 = jnp.float32
BF16 = jnp.bfloat16
HBM = pl.BlockSpec(memory_space=pltpu.HBM)
ANYWHERE = pl.BlockSpec(memory_space=pl.ANY)
SCALAR = pl.BlockSpec(memory_space=pltpu.SMEM)
LOCAL = pl.BlockSpec(memory_space=pltpu.VMEM)
LIMIT = pltpu.CompilerParams(vmem_limit_bytes=20 * 2**20)
WIDE = pltpu.CompilerParams(vmem_limit_bytes=57 * 2**20)


def rope_tables():
    freq = rope_base ** (-np.arange(64, dtype=np.float64) * 2.0 / HD)
    sign = np.concatenate([-np.ones(64), np.ones(64)])

    def pair(pos):
        ang = np.concatenate([pos[:, None] * freq, pos[:, None] * freq], 1)
        return np.stack([np.cos(ang), np.sin(ang) * sign]).astype(np.float32)

    return pair(np.arange(SPANS) * float(SPAN)), pair(np.arange(SPAN) * 1.0)


def rotated(x, span, big_ref, small_ref):
    cb = big_ref[0, pl.ds(span, 1), :]
    sb = big_ref[1, pl.ds(span, 1), :]
    cs = small_ref[0]
    ss = small_ref[1]
    cos = cb * cs - sb * ss
    sin = sb * cs + cb * ss
    return x * cos + pltpu.roll(x, 64, 1) * sin


def own_spans(order_ref):
    me = lax.axis_index("ctx")
    a, b = order_ref[2 * me], order_ref[2 * me + 1]
    return jnp.where(a < b, 0, 1).astype(jnp.int32), jnp.minimum(a, b)


def bring(pairs_of_refs, sems, base):
    copies = [pltpu.make_async_copy(a, b, sems.at[base + t]) for t, (a, b) in enumerate(pairs_of_refs)]
    for copy in copies:
        copy.start()
    return copies


def project_kernel(
    order_ref, x_ref, wk_ref, wv_ref, wq_ref, big_ref, small_ref,
    kv_ref, q_ref, x_s, w_s, big_s, small_s, sems,
):
    slot, span = own_spans(order_ref)
    depth = x_s.shape[1] // CHUNKS
    copies = []
    for c in range(CHUNKS):
        part = pl.ds(c * depth, depth)
        copies.append(bring([
            (wk_ref.at[part, :], w_s.at[part, pl.ds(0, HD)]),
            (wv_ref.at[part, :], w_s.at[part, pl.ds(HD, HD)]),
            (wq_ref.at[part, :], w_s.at[part, pl.ds(2 * HD, 2 * HD)]),
            (x_ref.at[:, part], x_s.at[:, part]),
        ], sems, 4 * c))
    copies.append(bring([(big_ref, big_s), (small_ref, small_s)], sems, 4 * CHUNKS))
    y = jnp.zeros((2 * SPAN, 4 * HD), F32)
    for c in range(CHUNKS):
        for copy in copies[c]:
            copy.wait()
        part = slice(c * depth, (c + 1) * depth)
        y = y + jnp.dot(x_s[:, part], w_s[part, :], preferred_element_type=F32)
    for copy in copies[CHUNKS]:
        copy.wait()
    scale = HD ** (-0.5) * math.log2(math.e)

    for s in range(2):
        qs = s ^ slot
        here = jnp.where(qs == 0, span, SPANS - 1 - span)
        rows = slice(s * SPAN, (s + 1) * SPAN)
        to = pl.multiple_of(qs * 2 * SPAN, 2 * SPAN)
        kv_ref[pl.ds(to, SPAN), :] = rotated(y[rows, :HD], here, big_s, small_s).astype(BF16)
        for c in range(SPAN // HD):
            tile = y[s * SPAN + c * HD:s * SPAN + (c + 1) * HD, HD:2 * HD]
            kv_ref[pl.ds(to + SPAN + c * HD, HD), :] = tile.T.astype(BF16)
        for h in range(2):
            r = rotated(y[rows, (2 + h) * HD:(3 + h) * HD], here, big_s, small_s) * scale
            q_ref[qs, :, h * SPAN:(h + 1) * SPAN] = r.T.astype(BF16)


def project(order, states, w_key, w_value, w_query, tables):
    rows, width = states.shape
    return pl.pallas_call(
        project_kernel,
        in_specs=[SCALAR] + [HBM] * 6,
        out_specs=[LOCAL] * 2,
        out_shape=[
            jax.ShapeDtypeStruct((4 * SPAN, HD), BF16),
            jax.ShapeDtypeStruct((2, HD, 2 * SPAN), BF16),
        ],
        scratch_shapes=[
            pltpu.VMEM((rows, width), BF16),
            pltpu.VMEM((width, 4 * HD), BF16),
            *[pltpu.VMEM(t.shape, F32) for t in tables],
            pltpu.SemaphoreType.DMA((4 * CHUNKS + 2,)),
        ],
        compiler_params=WIDE,
        cost_estimate=pl.CostEstimate(flops=rows * width * 8 * HD, bytes_accessed=13 * 2**20, transcendentals=0),
    )(order, states, w_key, w_value, w_query, *tables)


def attn_kernel(many, units, asked, begins, ends, order_ref, start_ref, *refs):
    n = len(units)
    kv = refs[:many]
    q_ref = refs[many]
    at = many + 1
    before = {}
    for qs in asked:
        if qs not in begins:
            before[qs] = refs[at:at + 2]
            at += 2
    outs = {}
    for qs in asked:
        wide = 1 if qs in ends else 2
        outs[qs] = refs[at:at + wide]
        at += wide
    kb, vb, m_ref, acc_ref, span_ref, sems = refs[at:]
    me = lax.axis_index("ctx")
    x0, z0, c0 = me // 8, (me // 2) % 4, me % 2
    own = own_spans(order_ref)[1]

    for t, (src, base, where, late, _) in enumerate(units):
        pltpu.make_async_copy(kv[src].at[pl.ds(base, SPAN), :], kb.at[t], sems.at[t, 0]).start()
        for c in range(4):
            pltpu.make_async_copy(
                kv[src].at[pl.ds(base + SPAN + c * HD, HD), :],
                vb.at[t, pl.ds(0, HD), pl.ds(c * HD, HD)],
                sems.at[t, 1 + c],
            ).start()
        if isinstance(where, tuple):
            dx, dz, dc = where
            who = ((x0 ^ dx) * 4 + ((z0 + dz + 4) % 4)) * 2 + (c0 ^ dc)
        else:
            who = where
        early = jnp.minimum(order_ref[2 * who], order_ref[2 * who + 1])
        span = SPANS - 1 - early if late else early
        if not isinstance(where, tuple):
            span = jnp.where(me == who, SPANS, span)
        span_ref[t] = span
    vb[:, HD:, :] = jnp.ones((n, 16, SPAN), BF16)
    for qs in asked:
        if qs in begins:
            m_ref[qs] = jnp.full(m_ref.shape[1:], neg_large, F32)
            acc_ref[qs] = jnp.zeros(acc_ref.shape[1:], F32)
        else:
            m_ref[qs] = before[qs][0][...]
            acc_ref[qs] = before[qs][1][...]

    def first_of(p):
        low = jnp.int32(0)
        for d in range(3):
            s = start_ref[d]
            low = jnp.where(s <= p, s, low)
        return low

    def block(u, qs, masked):
        k = kb[u]
        v = vb[u]
        qspan = SPANS - 1 - own if qs else own
        wide = 256
        parts = [slice(c * wide, (c + 1) * wide) for c in range(2 * SPAN // wide)]
        scores = [jnp.dot(k, q_ref[qs, :, sl], preferred_element_type=F32) for sl in parts]
        weights, factors = [], []
        for s, sl in zip(scores, parts):
            if masked:
                qpos = lax.broadcasted_iota(jnp.int32, (1, wide), 1) + (sl.start % SPAN + qspan * SPAN)
                low = first_of(qpos)
                kpos = lax.broadcasted_iota(jnp.int32, (SPAN, 1), 0) + span_ref[u] * SPAN
                s = jnp.where((kpos <= qpos) & (kpos >= low), s, neg_large)
            old = m_ref[qs, :, sl]
            new = jnp.maximum(old, jnp.max(s, 0, keepdims=True))
            weights.append(jnp.exp2(s - new).astype(BF16))
            factors.append(jnp.exp2(old - new))
            m_ref[qs, :, sl] = new
        for p, f, sl in zip(weights, factors, parts):
            acc_ref[qs, :, sl] = acc_ref[qs, :, sl] * f + jnp.dot(v, p, preferred_element_type=F32)

    def visit(u, qs):
        qspan = SPANS - 1 - own if qs else own
        kspan = span_ref[u]
        low_first = first_of(qspan * SPAN)
        low_last = first_of(qspan * SPAN + SPAN - 1)
        seen = (kspan <= qspan) & (kspan * SPAN + SPAN - 1 >= low_first)
        cut = (kspan == qspan) | (kspan * SPAN < low_last)

        @pl.when(seen & cut)
        def _():
            block(u, qs, True)

        @pl.when(seen & jnp.logical_not(cut))
        def _():
            block(u, qs, False)

    def steps(first, last, who):
        def step(u, carry):
            pltpu.make_async_copy(kb.at[u], kb.at[u], sems.at[u, 0]).wait()
            for c in range(4):
                spot = vb.at[u, pl.ds(0, HD), pl.ds(c * HD, HD)]
                pltpu.make_async_copy(spot, spot, sems.at[u, 1 + c]).wait()
            for qs in who:
                visit(u, qs)
            return carry

        lax.fori_loop(first, last, step, 0)

    t = 0
    while t < n:
        e = t
        while e < n and units[e][4] == units[t][4]:
            e += 1
        steps(t, e, units[t][4])
        t = e

    for qs in asked:
        if qs in ends:
            for h in range(2):
                sl = slice(h * SPAN, (h + 1) * SPAN)
                value = acc_ref[qs, 0:HD, sl] / acc_ref[qs, HD:HD + 1, sl]
                outs[qs][0][:, h * HD:(h + 1) * HD] = value.T.astype(BF16)
        else:
            outs[qs][0][...] = m_ref[qs]
            outs[qs][1][...] = acc_ref[qs]


def attend(order, starts, arrays, units, q, states, ends=()):
    n = len(units)
    many = len(arrays)
    asked = tuple(sorted(states))
    begins = tuple(s for s in asked if states[s] is None)
    inner = []
    shapes = []
    for s in asked:
        if s not in begins:
            inner += list(states[s])
        if s in ends:
            shapes.append(jax.ShapeDtypeStruct((SPAN, 2 * HD), BF16))
        else:
            shapes.append(jax.ShapeDtypeStruct((1, 2 * SPAN), F32))
            shapes.append(jax.ShapeDtypeStruct((HD + 16, 2 * SPAN), F32))
    work = sum(len(u[4]) for u in units)
    got = pl.pallas_call(
        functools.partial(attn_kernel, many, units, asked, begins, ends),
        in_specs=[SCALAR, SCALAR] + [ANYWHERE] * many + [LOCAL] * (1 + len(inner)),
        out_specs=[LOCAL] * len(shapes),
        out_shape=shapes,
        scratch_shapes=[
            pltpu.VMEM((n, SPAN, HD), BF16),
            pltpu.VMEM((n, HD + 16, SPAN), BF16),
            pltpu.VMEM((2, 1, 2 * SPAN), F32),
            pltpu.VMEM((2, HD + 16, 2 * SPAN), F32),
            pltpu.SMEM((n,), jnp.int32),
            pltpu.SemaphoreType.DMA((n, 5)),
        ],
        compiler_params=LIMIT,
        cost_estimate=pl.CostEstimate(
            flops=work * 10**6, bytes_accessed=n * 2**10, transcendentals=work * 2**10
        ),
    )(order, starts, *arrays, q, *inner)
    out = {}
    at = 0
    for s in asked:
        if s in ends:
            out[s] = got[at]
            at += 1
        else:
            out[s] = (got[at], got[at + 1])
            at += 2
    return out


def out_kernel(first, *refs):
    parts, w_ref, straight, crossed, out_ref, w_s, sems = refs[0:4], refs[4], refs[5:8], refs[8:11], *refs[11:]
    head = lax.axis_index("head").astype(jnp.int32)
    core = lax.axis_index("ctx") % 2
    cols = out_ref.shape[1]
    block = head + 1 - 2 * (head % 2) if first else head
    at = pl.multiple_of(block * cols, cols)
    own = pltpu.make_async_copy(w_ref.at[:, pl.ds(at, cols)], w_s.at[0], sems.at[0])
    own.start()

    def fetch(source):
        for t in range(3):
            pltpu.make_async_copy(source[t], w_s.at[1 + t], sems.at[1 + t]).start()

    use_straight = core == (1 if first else 0)

    @pl.when(use_straight)
    def _():
        fetch(straight)

    @pl.when(jnp.logical_not(use_straight))
    def _():
        fetch(crossed)

    total = None
    for t in range(4):
        pltpu.make_async_copy(w_s.at[t], w_s.at[t], sems.at[t]).wait()
        part = jnp.dot(parts[t][...], w_s[t], preferred_element_type=F32)
        total = part if total is None else total + part
    out_ref[...] = total.astype(out_ref.dtype)


def output(parts, straight, crossed, w_out, first):
    cols = w_out.shape[1] // 8
    return pl.pallas_call(
        functools.partial(out_kernel, first),
        in_specs=[LOCAL] * 4 + [ANYWHERE] * 7,
        out_specs=LOCAL,
        out_shape=jax.ShapeDtypeStruct((SPAN, cols), BF16 if first else F32),
        scratch_shapes=[pltpu.VMEM((4, 2 * HD, cols), BF16), pltpu.SemaphoreType.DMA((4,))],
        compiler_params=LIMIT,
        cost_estimate=pl.CostEstimate(flops=2**10, bytes_accessed=2**10, transcendentals=0),
    )(*parts, w_out, *straight, *crossed)


def join_kernel(order_ref, own0, other0, own1, other1, out_ref):
    slot = own_spans(order_ref)[0]
    for qs, (own, other) in enumerate(((own0, other0), (own1, other1))):
        row = pl.multiple_of((slot ^ qs) * SPAN, SPAN)
        out_ref[pl.ds(row, SPAN), :] = (own[...] + other[...].astype(F32)).astype(BF16)


def join(order, own, other):
    cols = own[0].shape[1]
    return pl.pallas_call(
        join_kernel,
        in_specs=[SCALAR] + [LOCAL] * 4,
        out_specs=LOCAL,
        out_shape=jax.ShapeDtypeStruct((2 * SPAN, cols), BF16),
        compiler_params=LIMIT,
        cost_estimate=pl.CostEstimate(flops=2 * SPAN * cols, bytes_accessed=4 * 2**20, transcendentals=0),
    )(order, own[0], other[0], own[1], other[1])


def pairs(move):
    def flat(x, y, z, c):
        x, y, z, c = x % 4, y % 4, z % 4, c % 2
        return ((x % 2 * 4 + z) * 2 + c) * 8 + y * 2 + x // 2

    return [
        (flat(x, y, z, c), flat(*move(x, y, z, c)))
        for x in range(4) for y in range(4) for z in range(4) for c in range(2)
    ]


to_pair = pairs(lambda x, y, z, c: (x ^ 1, y, z, c))
to_far = pairs(lambda x, y, z, c: (x + 2, y, z, c))
to_core = pairs(lambda x, y, z, c: (x, y, z, c + 1))
z_up = pairs(lambda x, y, z, c: (x, y, z + 1, c))
z_down = pairs(lambda x, y, z, c: (x, y, z - 1, c))
y_up = pairs(lambda x, y, z, c: (x, y + 1, z, c))
y_down = pairs(lambda x, y, z, c: (x, y - 1, z, c))
y_two = pairs(lambda x, y, z, c: (x, y + 2, z, c))


def send(value, to):
    return lax.ppermute(value, ("ctx", "head"), to)


def after(values, *others):
    return lax.optimization_barrier((values, others))[0]


def per_device(states, seg_ids, span_order, w_query, w_key, w_value, w_out):
    head = lax.axis_index("head").astype(jnp.int32)
    core = lax.axis_index("ctx").astype(jnp.int32) % 2
    y, far = head // 2, head % 2
    starts = jnp.sum(seg_ids[None, :] < jnp.arange(1, 4, dtype=jnp.int32)[:, None], 1, dtype=jnp.int32)
    tables = tuple(jnp.asarray(t) for t in rope_tables())

    rels = {
        "own": (0, 0), "pair": (1, 0), "below": (0, -1), "above": (0, 1),
        "pair_below": (1, -1), "pair_above": (1, 1), "two": (0, 2), "far": (1, 2),
    }
    held = {}

    def hold(name, crossed, array):
        for late in (0, 1):
            held[name, late, crossed] = (array, late * 2 * SPAN)

    def across_cores(names, *others):
        values = tuple(held[name, 0, 0][0] for name in names)
        for name, value in zip(names, after(values, *others) if others else values):
            hold(name, 1, send(value, to_core))

    def stage(picks, state, ends=()):
        arrays, units, index = [], [], {}
        for names, late, who in picks:
            for name in names:
                for c in (0, 1):
                    array, row = held[name, late, c]
                    if id(array) not in index:
                        index[id(array)] = len(arrays)
                        arrays.append(array)
                    units.append((index[id(array)], row, (*rels[name], c), late, who))
        return attend(span_order, starts, arrays, tuple(units), q, state, ends)

    own, q = project(span_order, states, w_key, w_value, w_query, tables)
    hold("own", 0, own)
    below, above, pair = send(own, z_up), send(own, z_down), send(own, to_pair)
    across_cores(("own",))

    half = w_out.shape[1] // 8

    def columns(step):
        block = 2 * ((y + step) % 4) + (far ^ core)
        return lax.dynamic_slice_in_dim(w_out, block * half, half, 1)

    straight = [send(columns(1), y_up), send(columns(3), y_down), send(columns(2), y_two)]
    both, ql, qe = (0, 1), (1,), (0,)
    s = stage([(("own",), 0, both), (("own",), 1, ql)], {0: None, 1: None})
    below, pair, above, straight = after((below, pair, above, straight), s)
    hold("below", 0, below)
    hold("above", 0, above)
    hold("pair", 0, pair)
    two = send(below, z_up)
    pair_above = send(pair, z_down)
    pair_below = send(below, to_pair)
    near = ("below", "above", "pair")
    across_cores(near)
    s = stage([(near, 0, both), (near, 1, ql)], s)
    two, pair_above, pair_below = after((two, pair_above, pair_below), s)
    hold("two", 0, two)
    hold("pair_above", 0, pair_above)
    hold("pair_below", 0, pair_below)
    far_early = send(pair_below[:2 * SPAN], z_up)
    far_late = send(pair_above[2 * SPAN:], z_down)
    rest = ("two", "pair_above", "pair_below")
    across_cores(rest)
    s = stage([(rest, 0, both)], s)
    far_early, far_late, straight = after((far_early, far_late, straight), s)
    for late, array in ((0, far_early), (1, far_late)):
        held["far", late, 0] = (array, 0)
        held["far", late, 1] = (send(array, to_core), 0)
    crossed = [send(w, to_core) for w in straight]
    early = stage([(("far",), 0, qe)], {0: after(s[0], far_late)}, qe)[0]
    early_moved = [send(early, y_up), send(early, y_down), send(early, y_two)]
    late = stage(
        [(("far",), 0, ql), (rest, 1, ql), (("far",), 1, ql)], {1: after(s[1], early, crossed)}, ql
    )[1]
    late_moved = [send(late, y_up), send(late, y_down), send(late, y_two)]

    early_parts = [early, *after(early_moved, late)]
    early_theirs = output(early_parts, straight, crossed, w_out, True)
    early_other = send(early_theirs, to_far)
    late_parts = [late, *after(late_moved, early_theirs)]
    late_theirs = output(late_parts, straight, crossed, w_out, True)
    late_other = send(late_theirs, to_far)
    early_own = output(after(early_parts, late_theirs, early_other), straight, crossed, w_out, False)
    late_own = output(after(late_parts, late_theirs, early_other), straight, crossed, w_out, False)
    return join(span_order, [early_own, late_own], [early_other, late_other])


def solution(mesh):
    in_specs = (
        P("ctx", None),
        P(),
        P(),
        P(None, "head"),
        P(None, "head"),
        P(None, "head"),
        P("head", None),
    )
    out_specs = P("ctx", "head")
    return jax.shard_map(
        per_device, mesh=mesh, in_specs=in_specs, out_specs=out_specs, check_vma=False
    )
```
